128 devices in a mesh: row: 4 (over x_hi, core), pair: 32 (over y, z, x_lo).
Axes of the slice: x: 4 (x_hi: 2, x_lo: 2; x = x_hi * 2 + x_lo), y: 4, z: 4, core: 2. Of those that a mesh axis runs over, the one named last changes fastest.
Arguments:
- samples: bfloat16 [32768, 16384], P(('row', 'pair')), may hold values from -6 to 6
Outputs:
- rotated: bfloat16 [32768, 16384], P('row', 'pair')
The draws below stay inside these ranges and needn't reach their ends.
All inputs are finite; a program needn't handle non-finite values.
Results may differ from the reference program's by a relative error of at most 0.0046.
Values may be sent and summed in bfloat16 or wider, within the bound.
A program may use at most 128 MiB of HBM per device.

```python
import jax
import jax.numpy as jnp
from jax import lax

BLOCK = 256
NS_STEPS = 5
ROWS = 32768
FEAT = 16384


def steps_of(stream_key, shape, cuts, least, high):
    def one(position, shards_of):
        heights = jax.random.uniform(jax.random.fold_in(jax.random.fold_in(stream_key, 6), position), (shards_of,), jnp.float32, least / len(cuts), high / len(cuts))
        return jnp.repeat(jnp.exp(heights), shape[position] // shards_of).reshape((-1,) + (1,) * (len(shape) - position - 1))

    loudness = one(*cuts[0])
    for cut in cuts[1:]:
        loudness = loudness * one(*cut)
    return loudness


def scatter_about(key, extent, scale, limit, pieces=(), kind=jnp.bfloat16):
    drawn = jax.random.normal(key, extent, jnp.float32) * scale
    if len(pieces) > 0:
        drawn = steps_of(key, extent, pieces, -0.22, 0.18) * drawn
    return jnp.clip(drawn, min=-limit, max=limit).astype(kind)


def setup_inputs(seed: int = 0) -> dict:
    streams_of = jax.random.split(jax.random.key(seed), 2)
    samples = scatter_about(streams_of[0], (ROWS, FEAT), 1.0, 6.0, ((0, 128),))
    return dict(samples=samples)


def newton_steps(scaled):
    width = scaled.shape[0]
    eye_mat = jnp.eye(width, dtype=jnp.float32)
    matrix_m = scaled
    inverse_z = eye_mat
    for step in range(NS_STEPS):
        factor_s = 1.5 * eye_mat - 0.5 * jnp.dot(inverse_z, matrix_m, precision=lax.Precision.HIGHEST)
        matrix_m = jnp.dot(matrix_m, factor_s, precision=lax.Precision.HIGHEST)
        inverse_z = jnp.dot(factor_s, inverse_z, precision=lax.Precision.HIGHEST)
    return inverse_z

def one_pair(pair_cols):
    gram_matrix = jnp.dot(pair_cols.T, pair_cols, preferred_element_type=jnp.float32)
    frobenius = jnp.sqrt(jnp.sum(gram_matrix * gram_matrix))
    inverse_z = newton_steps(gram_matrix / frobenius)
    rotation = (inverse_z * jnp.sqrt(ROWS / frobenius)).astype(jnp.bfloat16)
    return jnp.dot(pair_cols, rotation, preferred_element_type=jnp.float32).astype(jnp.bfloat16)

def reference(samples):
    pair_count = FEAT // (2 * BLOCK)
    stacked = samples.reshape(ROWS, pair_count, 2 * BLOCK).transpose(1, 0, 2)
    results = lax.map(one_pair, stacked)
    left_blocks = results[:, :, :BLOCK]
    right_blocks = jnp.roll(results[:, :, BLOCK:], 1, axis=0)
    joined = jnp.concatenate([left_blocks, right_blocks], axis=2)
    return joined.transpose(1, 0, 2).reshape(ROWS, FEAT)
```

```python
import functools

import jax
import jax.numpy as jnp
from jax import lax
from jax.experimental import pallas as pl
from jax.experimental.pallas import tpu as pltpu
from jax.sharding import PartitionSpec as P

MESH = pl.DeviceIdType.MESH
F32 = jnp.float32
BF16 = jnp.bfloat16
NS_STEPS = 5
ROWS = 32768
CHIPS = 16
PEERS = CHIPS - 1
SUBS = 4
CHUNK = 64
PAIR = 512
HALF = 256
PACKED = 3 * HALF
CORE_PART = PACKED // 2
QUARTER = CORE_PART // 4
SENDS = 2 * SUBS * PEERS


def dot(left, right, dims=((1,), (0,))):
    return lax.dot_general(left, right, (dims, ((), ())), preferred_element_type=F32)


def split(ref_hi, ref_lo, value):
    high = value.astype(BF16)
    ref_hi[...] = high
    ref_lo[...] = (value - high.astype(F32)).astype(BF16)


def product(left, right):
    lh, ll = left
    rh, rl = right
    return dot(lh[...], rh[...]) + (dot(lh[...], rl[...]) + dot(ll[...], rh[...]))


def kernel(
    x_ref, o_ref,
    y, part, from_core, from_quarter, full, zmat, mmat, zh, zl, mh, ml, th, tl, rot, w_send, w_keep,
    own_sem, a2a_send, a2a_recv, core_send, core_recv, rs_send, rs_recv, ag_send, ag_recv,
    back_send, back_recv, w_send_sem, w_recv_sem, w_keep_sem,
):
    row = lax.axis_index("row")
    pair = lax.axis_index("pair")
    core = lax.rem(row, 2)
    x_hi = row // 2
    plane = lax.rem(pair, 2)
    chip = pair // 2
    y_pos, z_pos = chip // 4, lax.rem(chip, 4)
    quarter = x_hi * 2 + plane

    def member(stage, step):
        other = lax.rem(quarter + step, 4)
        other_plane = lax.rem(other, 2)
        other_chip = chip
        if stage == 1:
            other_chip = lax.rem(chip + plane - other_plane + CHIPS, CHIPS)
        return other, ((other // 2) * 2 + core, other_chip * 2 + other_plane)

    core_peer = (x_hi * 2 + 1 - core, pair)

    def partner(stage):
        other_chip = chip
        if stage == 1:
            other_chip = lax.rem(chip + 2 * plane - 1 + CHIPS, CHIPS)
        return (row, other_chip * 2 + 1 - plane)

    barrier = pltpu.get_barrier_semaphore()

    def greet(device):
        pl.semaphore_signal(barrier, inc=1, device_id=device, device_id_type=MESH)

    def offset(i):
        turn = 1 + lax.rem(i * 7, PEERS)
        return lax.rem(y_pos + turn // 4, 4) * 4 + lax.rem(z_pos + lax.rem(turn, 4), 4)

    def greet_plane(i, carry):
        greet((row, offset(i) * 2 + plane))
        return carry

    lax.fori_loop(0, PEERS, greet_plane, 0)
    greet(core_peer)
    for step in range(1, 4):
        greet(member(0, step)[1])
    greet(member(1, 1)[1])
    greet(member(1, 3)[1])

    def columns_of(stage, target):
        index = 2 * target
        if not isinstance(stage, int):
            index = index + stage * (2 * plane - 1)
        elif stage == 1:
            index = index + 2 * plane - 1
        index = lax.rem(index + 2 * CHIPS, 2 * CHIPS)
        return pl.ds(pl.multiple_of(index * PAIR, PAIR), PAIR)

    def own_copy(stage):
        return pltpu.make_async_copy(
            x_ref.at[:, :, columns_of(stage, chip)], y.at[stage, :, chip], own_sem.at[stage]
        )

    for stage in range(2):
        own_copy(stage).start()
    pl.semaphore_wait(barrier, PEERS + 6)

    def a2a_copy(n):
        phase, i = n // PEERS, lax.rem(n, PEERS)
        stage, sub = phase // SUBS, lax.rem(phase, SUBS)
        target = offset(i)
        return pltpu.make_async_remote_copy(
            src_ref=x_ref.at[sub, :, columns_of(stage, target)],
            dst_ref=y.at[stage, sub, chip],
            send_sem=a2a_send.at[i],
            recv_sem=a2a_recv.at[phase],
            device_id=(row, target * 2 + plane),
            device_id_type=MESH,
        )

    def a2a_first(n, carry):
        a2a_copy(n).start()
        return carry

    def a2a_next(n, carry):
        a2a_copy(n - PEERS).wait_send()
        a2a_copy(n).start()
        return carry

    sent = [0]

    def pump(count):
        stop = min(SENDS, sent[0] + count)
        if stop > sent[0]:
            lax.fori_loop(sent[0], stop, a2a_next, 0)
            sent[0] = stop

    def a2a_arrived(stage, sub):
        landed = y.at[stage, sub, pl.ds(0, PEERS)]
        pltpu.make_async_copy(landed, landed, a2a_recv.at[stage * SUBS + sub]).wait()

    def gram(stage, sub):
        rows = y[stage, sub].reshape(CHIPS * CHUNK, PAIR)
        left, right = rows[:, :HALF], rows[:, HALF:]
        for index, (one, two) in enumerate(((left, left), (left, right), (right, right))):
            here = pl.ds(index * HALF, HALF)
            term = dot(one, two, ((0,), (0,)))
            if sub == 0:
                part[stage, here] = term
            else:
                part[stage, here] += term

    core_rows = pl.ds(pl.multiple_of(core * CORE_PART, CORE_PART), CORE_PART)
    peer_rows = pl.ds(pl.multiple_of((1 - core) * CORE_PART, CORE_PART), CORE_PART)

    def quarter_rows(which):
        return pl.ds(pl.multiple_of(core * CORE_PART + which * QUARTER, QUARTER), QUARTER)

    def core_copy(stage):
        return pltpu.make_async_remote_copy(
            src_ref=part.at[stage, peer_rows], dst_ref=from_core.at[stage],
            send_sem=core_send.at[stage], recv_sem=core_recv.at[stage],
            device_id=core_peer, device_id_type=MESH,
        )

    def rs_copy(stage, step):
        other, device = member(stage, step)
        return pltpu.make_async_remote_copy(
            src_ref=part.at[stage, quarter_rows(other)], dst_ref=from_quarter.at[stage, step - 1],
            send_sem=rs_send.at[stage, step - 1], recv_sem=rs_recv.at[stage, step - 1],
            device_id=device, device_id_type=MESH,
        )

    def ag_copy(stage, step):
        _, device = member(stage, step)
        return pltpu.make_async_remote_copy(
            src_ref=full.at[stage, quarter_rows(quarter)], dst_ref=full.at[stage, quarter_rows(quarter)],
            send_sem=ag_send.at[stage, step - 1], recv_sem=ag_recv.at[stage, step - 1],
            device_id=device, device_id_type=MESH,
        )

    def back_copy(stage):
        return pltpu.make_async_remote_copy(
            src_ref=full.at[stage, core_rows], dst_ref=full.at[stage, core_rows],
            send_sem=back_send.at[stage], recv_sem=back_recv.at[stage],
            device_id=core_peer, device_id_type=MESH,
        )

    def reduce_1(stage):
        core_copy(stage).start()

    def reduce_2(stage):
        core_copy(stage).wait_recv()
        part[stage, core_rows] += from_core[stage]
        for step in (2, 1, 3):
            rs_copy(stage, step).start()

    def reduce_3(stage):
        total = part[stage, quarter_rows(quarter)]
        for step in (1, 3, 2):
            rs_copy(stage, step).wait_recv()
            total = total + from_quarter[stage, step - 1]
        full[stage, quarter_rows(quarter)] = total
        for step in (2, 1, 3):
            ag_copy(stage, step).start()

    def reduce_4(stage):
        for step in (1, 3, 2):
            ag_copy(stage, step).wait_recv()
        back_copy(stage).start()

    def reduce_5(stage):
        back_copy(stage).wait_recv()
        for step in range(1, 4):
            rs_copy(stage, step).wait_send()
            ag_copy(stage, step).wait_send()
        core_copy(stage).wait_send()
        back_copy(stage).wait_send()

    diagonal = lambda: (
        lax.broadcasted_iota(jnp.int32, (PAIR, PAIR), 0) == lax.broadcasted_iota(jnp.int32, (PAIR, PAIR), 1)
    ).astype(F32)

    def newton(stage, between):
        g00 = full[stage, pl.ds(0, HALF)]
        g01 = full[stage, pl.ds(HALF, HALF)]
        g11 = full[stage, pl.ds(2 * HALF, HALF)]
        square = (
            jnp.sum(g00 * g00, keepdims=True) + 2.0 * jnp.sum(g01 * g01, keepdims=True)
            + jnp.sum(g11 * g11, keepdims=True)
        )
        norm = jnp.sqrt(square)
        mmat[:HALF, :HALF] = g00 / norm
        mmat[:HALF, HALF:] = g01 / norm
        mmat[HALF:, :HALF] = (g01 / norm).T
        mmat[HALF:, HALF:] = g11 / norm
        split(mh, ml, mmat[...])
        zmat[...] = 1.5 * diagonal() - 0.5 * mmat[...]
        mmat[...] = 1.5 * mmat[...] - 0.5 * product((mh, ml), (mh, ml))
        split(zh, zl, zmat[...])
        split(mh, ml, mmat[...])
        between()
        for _ in range(NS_STEPS - 2):
            split(th, tl, product((zh, zl), (mh, ml)))
            mmat[...] = 1.5 * mmat[...] - 0.5 * product((mh, ml), (th, tl))
            zmat[...] = 1.5 * zmat[...] - 0.5 * product((th, tl), (zh, zl))
            split(zh, zl, zmat[...])
            split(mh, ml, mmat[...])
            between()
        split(th, tl, product((zh, zl), (mh, ml)))
        last = 1.5 * zmat[...] - 0.5 * product((th, tl), (zh, zl))
        rot[stage] = (last * jnp.sqrt(ROWS / norm)).astype(BF16)

    def half_of(stage, kept):
        which = plane if (stage == 0) == kept else 1 - plane
        return pl.ds(pl.multiple_of(which * HALF, HALF), HALF)

    def send_copy(stage, sub):
        return pltpu.make_async_remote_copy(
            src_ref=w_send.at[stage, sub],
            dst_ref=o_ref.at[:, plane, sub, :, half_of(stage, False)],
            send_sem=w_send_sem.at[stage, sub], recv_sem=w_recv_sem.at[stage, sub],
            device_id=partner(stage), device_id_type=MESH,
        )

    def keep_copy(stage, sub):
        return pltpu.make_async_copy(
            w_keep.at[stage, sub],
            o_ref.at[:, plane, sub, :, half_of(stage, True)],
            w_keep_sem.at[stage, sub],
        )

    def apply(stage, sub, kept):
        rows = y[stage, sub].reshape(CHIPS * CHUNK, PAIR)
        value = dot(rows, rot[stage, :, half_of(stage, kept)]).astype(BF16)
        (w_keep if kept else w_send)[stage, sub] = value.reshape(CHIPS, CHUNK, HALF)
        (keep_copy if kept else send_copy)(stage, sub).start()

    lax.fori_loop(0, PEERS, a2a_first, 0)
    sent[0] = PEERS
    for sub in range(SUBS):
        pump(PEERS)
        if sub == 0:
            own_copy(0).wait()
        a2a_arrived(0, sub)
        gram(0, sub)
    reduce_1(0)
    pump(2)
    reduce_2(0)
    pump(4)
    reduce_3(0)
    pump(4)
    reduce_4(0)
    pump(3)
    reduce_5(0)
    newton(0, lambda: pump(3))
    for sub in range(SUBS):
        apply(0, sub, False)
    own_copy(1).wait()
    for sub in range(SUBS):
        if sub + SUBS + 1 < 2 * SUBS:
            pump((sub + SUBS + 2) * PEERS - sent[0])
        a2a_arrived(1, sub)
        gram(1, sub)
        if sub < SUBS - 1:
            apply(0, sub, True)
    reduce_1(1)
    apply(0, SUBS - 1, True)
    reduce_2(1)
    reduce_3(1)
    reduce_4(1)
    reduce_5(1)
    newton(1, lambda: None)
    for sub in range(SUBS):
        apply(1, sub, False)
    for sub in range(SUBS):
        apply(1, sub, True)

    def a2a_drain(n, carry):
        a2a_copy(n).wait_send()
        return carry

    lax.fori_loop(SENDS - PEERS, SENDS, a2a_drain, 0)
    for stage in range(2):
        for sub in range(SUBS):
            send_copy(stage, sub).wait()
            keep_copy(stage, sub).wait()


def body(samples):
    sems = lambda *shape: pltpu.SemaphoreType.DMA(shape)
    square = (PAIR, PAIR)
    out = pl.pallas_call(
        kernel,
        out_shape=jax.ShapeDtypeStruct((CHIPS, 2, SUBS, CHUNK, PAIR), BF16),
        in_specs=[pl.BlockSpec(memory_space=pl.ANY)],
        out_specs=pl.BlockSpec(memory_space=pl.ANY),
        scratch_shapes=[
            pltpu.VMEM((2, SUBS, CHIPS, CHUNK, PAIR), BF16),
            pltpu.VMEM((2, PACKED, HALF), F32),
            pltpu.VMEM((2, CORE_PART, HALF), F32),
            pltpu.VMEM((2, 3, QUARTER, HALF), F32),
            pltpu.VMEM((2, PACKED, HALF), F32),
            pltpu.VMEM(square, F32), pltpu.VMEM(square, F32),
            *[pltpu.VMEM(square, BF16)] * 6,
            pltpu.VMEM((2, *square), BF16),
            pltpu.VMEM((2, SUBS, CHIPS, CHUNK, HALF), BF16),
            pltpu.VMEM((2, SUBS, CHIPS, CHUNK, HALF), BF16),
            sems(2), sems(PEERS), sems(2 * SUBS), sems(2), sems(2), sems(2, 3), sems(2, 3), sems(2, 3), sems(2, 3),
            sems(2), sems(2), sems(2, SUBS), sems(2, SUBS), sems(2, SUBS),
        ],
        compiler_params=pltpu.CompilerParams(
            collective_id=0, has_side_effects=True, vmem_limit_bytes=56 * 2**20
        ),
    )(samples.reshape(SUBS, CHUNK, samples.shape[1]))
    return out.reshape(-1, PAIR)


def solution(mesh):
    return jax.shard_map(
        body, mesh=mesh, in_specs=(P(("row", "pair"), None),), out_specs=P("row", "pair"), check_vma=False
    )
```

```python
import functools

import jax
import jax.numpy as jnp
from jax import lax
from jax.experimental import pallas as pl
from jax.experimental.pallas import tpu as pltpu
from jax.sharding import PartitionSpec as P

MESH = pl.DeviceIdType.MESH
F32 = jnp.float32
BF16 = jnp.bfloat16
NS_STEPS = 5
ROWS = 32768
CHIPS = 16
PEERS = CHIPS - 1
SUBS = 4
CHUNK = 64
PAIR = 512
HALF = 256
PACKED = 3 * HALF
CORE_PART = PACKED // 2
QUARTER = CORE_PART // 4
SENDS = 2 * SUBS * PEERS
WINDOW = SUBS * PEERS
SHARED = 2


def dot(left, right, dims=((1,), (0,))):
    return lax.dot_general(left, right, (dims, ((), ())), preferred_element_type=F32)


def split(ref_hi, ref_lo, value):
    high = value.astype(BF16)
    ref_hi[...] = high
    ref_lo[...] = (value - high.astype(F32)).astype(BF16)


def product(left, right, fine=True):
    lh, ll = left
    rh, rl = right
    if not fine:
        return dot(lh[...], rh[...])
    return dot(lh[...], rh[...]) + (dot(lh[...], rl[...]) + dot(ll[...], rh[...]))


def kernel(
    x_ref, o_ref,
    y, part, from_core, from_quarter, full, zmat, mmat, zh, zl, mh, ml, th, tl, rot, w_send, w_keep, shared, w_shared,
    own_sem, a2a_send, a2a_recv, core_send, core_recv, rs_send, rs_recv, ag_send, ag_recv,
    back_send, back_recv, w_send_sem, w_recv_sem, w_keep_sem, share_send, share_recv, w_shared_sem,
):
    row = lax.axis_index("row")
    pair = lax.axis_index("pair")
    core = lax.rem(row, 2)
    x_hi = row // 2
    plane = lax.rem(pair, 2)
    chip = pair // 2
    y_pos, z_pos = chip // 4, lax.rem(chip, 4)
    quarter = x_hi * 2 + plane

    def member(stage, step):
        other = lax.rem(quarter + step, 4)
        other_plane = lax.rem(other, 2)
        other_chip = chip
        if stage == 1:
            other_chip = lax.rem(chip + plane - other_plane + CHIPS, CHIPS)
        return other, ((other // 2) * 2 + core, other_chip * 2 + other_plane)

    core_peer = (x_hi * 2 + 1 - core, pair)

    def partner(stage):
        other_chip = chip
        if stage == 1:
            other_chip = lax.rem(chip + 2 * plane - 1 + CHIPS, CHIPS)
        return (row, other_chip * 2 + 1 - plane)

    barrier = pltpu.get_barrier_semaphore()

    def greet(device):
        pl.semaphore_signal(barrier, inc=1, device_id=device, device_id_type=MESH)

    def offset(i):
        turn = 1 + lax.rem(i * 7, PEERS)
        return lax.rem(y_pos + turn // 4, 4) * 4 + lax.rem(z_pos + lax.rem(turn, 4), 4)

    def greet_plane(i, carry):
        greet((row, offset(i) * 2 + plane))
        return carry

    lax.fori_loop(0, PEERS, greet_plane, 0)
    greet(core_peer)
    for step in range(1, 4):
        greet(member(0, step)[1])
    greet(member(1, 1)[1])
    greet(member(1, 3)[1])

    def columns_of(stage, target):
        index = 2 * target
        if not isinstance(stage, int):
            index = index + stage * (2 * plane - 1)
        elif stage == 1:
            index = index + 2 * plane - 1
        index = lax.rem(index + 2 * CHIPS, 2 * CHIPS)
        return pl.ds(pl.multiple_of(index * PAIR, PAIR), PAIR)

    def own_copy(stage):
        return pltpu.make_async_copy(
            x_ref.at[:, :, columns_of(stage, chip)], y.at[stage, :, chip], own_sem.at[stage]
        )

    for stage in range(2):
        own_copy(stage).start()
    pl.semaphore_wait(barrier, PEERS + 6)

    def a2a_copy(n):
        phase, i = n // PEERS, lax.rem(n, PEERS)
        stage, sub = phase // SUBS, lax.rem(phase, SUBS)
        target = offset(i)
        return pltpu.make_async_remote_copy(
            src_ref=x_ref.at[sub, :, columns_of(stage, target)],
            dst_ref=y.at[stage, sub, chip],
            send_sem=a2a_send.at[lax.rem(n, WINDOW)],
            recv_sem=a2a_recv.at[phase],
            device_id=(row, target * 2 + plane),
            device_id_type=MESH,
        )

    def a2a_first(n, carry):
        a2a_copy(n).start()
        return carry

    def a2a_next(n, carry):
        a2a_copy(n - WINDOW).wait_send()
        a2a_copy(n).start()
        return carry

    sent = [0]

    def pump(count):
        stop = min(SENDS, sent[0] + count)
        if stop > sent[0]:
            lax.fori_loop(sent[0], stop, a2a_next, 0)
            sent[0] = stop

    def a2a_arrived(stage, sub):
        landed = y.at[stage, sub, pl.ds(0, PEERS)]
        pltpu.make_async_copy(landed, landed, a2a_recv.at[stage * SUBS + sub]).wait()

    def gram(stage, sub):
        rows = y[stage, sub].reshape(CHIPS * CHUNK, PAIR)
        left, right = rows[:, :HALF], rows[:, HALF:]
        for index, (one, two) in enumerate(((left, left), (left, right), (right, right))):
            here = pl.ds(index * HALF, HALF)
            term = dot(one, two, ((0,), (0,)))
            if sub == 0:
                part[stage, here] = term
            else:
                part[stage, here] += term

    core_rows = pl.ds(pl.multiple_of(core * CORE_PART, CORE_PART), CORE_PART)
    peer_rows = pl.ds(pl.multiple_of((1 - core) * CORE_PART, CORE_PART), CORE_PART)

    def quarter_rows(which):
        return pl.ds(pl.multiple_of(core * CORE_PART + which * QUARTER, QUARTER), QUARTER)

    def core_copy(stage):
        return pltpu.make_async_remote_copy(
            src_ref=part.at[stage, peer_rows], dst_ref=from_core.at[stage],
            send_sem=core_send.at[stage], recv_sem=core_recv.at[stage],
            device_id=core_peer, device_id_type=MESH,
        )

    def rs_copy(stage, step):
        other, device = member(stage, step)
        return pltpu.make_async_remote_copy(
            src_ref=part.at[stage, quarter_rows(other)], dst_ref=from_quarter.at[stage, step - 1],
            send_sem=rs_send.at[stage, step - 1], recv_sem=rs_recv.at[stage, step - 1],
            device_id=device, device_id_type=MESH,
        )

    def ag_copy(stage, step):
        _, device = member(stage, step)
        return pltpu.make_async_remote_copy(
            src_ref=full.at[stage, quarter_rows(quarter)], dst_ref=full.at[stage, quarter_rows(quarter)],
            send_sem=ag_send.at[stage, step - 1], recv_sem=ag_recv.at[stage, step - 1],
            device_id=device, device_id_type=MESH,
        )

    def back_copy(stage):
        return pltpu.make_async_remote_copy(
            src_ref=full.at[stage, core_rows], dst_ref=full.at[stage, core_rows],
            send_sem=back_send.at[stage], recv_sem=back_recv.at[stage],
            device_id=core_peer, device_id_type=MESH,
        )

    def reduce_1(stage):
        core_copy(stage).start()

    def reduce_2(stage):
        core_copy(stage).wait_recv()
        part[stage, core_rows] += from_core[stage]
        for step in (2, 1, 3):
            rs_copy(stage, step).start()

    def reduce_3(stage):
        total = part[stage, quarter_rows(quarter)]
        for step in (1, 3, 2):
            rs_copy(stage, step).wait_recv()
            total = total + from_quarter[stage, step - 1]
        full[stage, quarter_rows(quarter)] = total
        for step in (2, 1, 3):
            ag_copy(stage, step).start()

    def reduce_4(stage):
        for step in (1, 3, 2):
            ag_copy(stage, step).wait_recv()
        back_copy(stage).start()

    def reduce_5(stage):
        back_copy(stage).wait_recv()
        for step in range(1, 4):
            rs_copy(stage, step).wait_send()
            ag_copy(stage, step).wait_send()
        core_copy(stage).wait_send()
        back_copy(stage).wait_send()

    diagonal = lambda: (
        lax.broadcasted_iota(jnp.int32, (PAIR, PAIR), 0) == lax.broadcasted_iota(jnp.int32, (PAIR, PAIR), 1)
    ).astype(F32)

    def newton(stage):
        g00 = full[stage, pl.ds(0, HALF)]
        g01 = full[stage, pl.ds(HALF, HALF)]
        g11 = full[stage, pl.ds(2 * HALF, HALF)]
        square = (
            jnp.sum(g00 * g00, keepdims=True) + 2.0 * jnp.sum(g01 * g01, keepdims=True)
            + jnp.sum(g11 * g11, keepdims=True)
        )
        norm = jnp.sqrt(square)
        mmat[:HALF, :HALF] = g00 / norm
        mmat[:HALF, HALF:] = g01 / norm
        mmat[HALF:, :HALF] = (g01 / norm).T
        mmat[HALF:, HALF:] = g11 / norm
        split(mh, ml, mmat[...])
        zmat[...] = 1.5 * diagonal() - 0.5 * mmat[...]
        mmat[...] = 1.5 * mmat[...] - 0.5 * product((mh, ml), (mh, ml), False)
        split(zh, zl, zmat[...])
        split(mh, ml, mmat[...])
        for step in range(1, NS_STEPS - 1):
            fine = step >= NS_STEPS - 2
            split(th, tl, product((zh, zl), (mh, ml), fine))
            mmat[...] = 1.5 * mmat[...] - 0.5 * product((mh, ml), (th, tl), fine)
            zmat[...] = 1.5 * zmat[...] - 0.5 * product((th, tl), (zh, zl), fine)
            split(zh, zl, zmat[...])
            split(mh, ml, mmat[...])
        split(th, tl, product((zh, zl), (mh, ml)))
        last = 1.5 * zmat[...] - 0.5 * product((th, tl), (zh, zl))
        rot[stage] = (last * jnp.sqrt(ROWS / norm)).astype(BF16)

    def half_of(stage, kept):
        which = plane if (stage == 0) == kept else 1 - plane
        return pl.ds(pl.multiple_of(which * HALF, HALF), HALF)

    def send_copy(stage, sub):
        return pltpu.make_async_remote_copy(
            src_ref=w_send.at[stage, sub],
            dst_ref=o_ref.at[:, plane, sub, :, half_of(stage, False)],
            send_sem=w_send_sem.at[stage, sub], recv_sem=w_recv_sem.at[stage, sub],
            device_id=partner(stage), device_id_type=MESH,
        )

    def keep_copy(stage, sub):
        return pltpu.make_async_copy(
            w_keep.at[stage, sub],
            o_ref.at[:, plane, sub, :, half_of(stage, True)],
            w_keep_sem.at[stage, sub],
        )

    def share_copy(sub):
        return pltpu.make_async_remote_copy(
            src_ref=y.at[0, sub], dst_ref=shared.at[sub],
            send_sem=share_send.at[sub], recv_sem=share_recv.at[sub],
            device_id=partner(0), device_id_type=MESH,
        )

    def shared_keep_copy(sub):
        return pltpu.make_async_copy(
            w_shared.at[sub],
            o_ref.at[:, 1 - plane, sub, :, half_of(0, True)],
            w_shared_sem.at[sub],
        )

    def apply_shared(sub):
        share_copy(sub).wait_recv()
        rows = shared[sub].reshape(CHIPS * CHUNK, PAIR)
        value = dot(rows, rot[0, :, half_of(0, True)]).astype(BF16)
        w_shared[sub] = value.reshape(CHIPS, CHUNK, HALF)
        shared_keep_copy(sub).start()

    def apply(stage, sub, kept):
        rows = y[stage, sub].reshape(CHIPS * CHUNK, PAIR)
        value = dot(rows, rot[stage, :, half_of(stage, kept)]).astype(BF16)
        (w_keep if kept else w_send)[stage, sub] = value.reshape(CHIPS, CHUNK, HALF)
        (keep_copy if kept else send_copy)(stage, sub).start()

    lax.fori_loop(0, WINDOW, a2a_first, 0)
    sent[0] = WINDOW
    for sub in range(SUBS):
        pump(PEERS)
        if sub == 0:
            own_copy(0).wait()
        a2a_arrived(0, sub)
        if sub < SHARED:
            share_copy(sub).start()
        gram(0, sub)
    reduce_1(0)
    reduce_2(0)
    reduce_3(0)
    reduce_4(0)
    reduce_5(0)
    newton(0)
    apply(0, 2, False)
    own_copy(1).wait()
    for sub in range(SUBS):
        a2a_arrived(1, sub)
        gram(1, sub)
        if sub < SUBS - 1:
            apply(0, sub, True)
    reduce_1(1)
    apply(0, SUBS - 1, True)
    reduce_2(1)
    apply_shared(0)
    reduce_3(1)
    apply(0, 3, False)
    apply_shared(1)
    reduce_4(1)
    reduce_5(1)
    newton(1)
    for sub in range(SUBS):
        apply(1, sub, False)
    for sub in range(SUBS):
        apply(1, sub, True)

    def a2a_drain(n, carry):
        a2a_copy(n).wait_send()
        return carry

    lax.fori_loop(SENDS - WINDOW, SENDS, a2a_drain, 0)
    for stage in range(2):
        for sub in range(SUBS):
            if stage == 1 or sub >= SHARED:
                send_copy(stage, sub).wait()
            keep_copy(stage, sub).wait()
    for sub in range(SHARED):
        share_copy(sub).wait_send()
        shared_keep_copy(sub).wait()


def body(samples):
    sems = lambda *shape: pltpu.SemaphoreType.DMA(shape)
    square = (PAIR, PAIR)
    out = pl.pallas_call(
        kernel,
        out_shape=jax.ShapeDtypeStruct((CHIPS, 2, SUBS, CHUNK, PAIR), BF16),
        in_specs=[pl.BlockSpec(memory_space=pl.ANY)],
        out_specs=pl.BlockSpec(memory_space=pl.ANY),
        scratch_shapes=[
            pltpu.VMEM((2, SUBS, CHIPS, CHUNK, PAIR), BF16),
            pltpu.VMEM((2, PACKED, HALF), F32),
            pltpu.VMEM((2, CORE_PART, HALF), F32),
            pltpu.VMEM((2, 3, QUARTER, HALF), F32),
            pltpu.VMEM((2, PACKED, HALF), F32),
            pltpu.VMEM(square, F32), pltpu.VMEM(square, F32),
            *[pltpu.VMEM(square, BF16)] * 6,
            pltpu.VMEM((2, *square), BF16),
            pltpu.VMEM((2, SUBS, CHIPS, CHUNK, HALF), BF16),
            pltpu.VMEM((2, SUBS, CHIPS, CHUNK, HALF), BF16),
            pltpu.VMEM((SHARED, CHIPS, CHUNK, PAIR), BF16),
            pltpu.VMEM((SHARED, CHIPS, CHUNK, HALF), BF16),
            sems(2), sems(WINDOW), sems(2 * SUBS), sems(2), sems(2), sems(2, 3), sems(2, 3), sems(2, 3), sems(2, 3),
            sems(2), sems(2), sems(2, SUBS), sems(2, SUBS), sems(2, SUBS),
            sems(SHARED), sems(SHARED), sems(SHARED),
        ],
        compiler_params=pltpu.CompilerParams(
            collective_id=0, has_side_effects=True, vmem_limit_bytes=56 * 2**20
        ),
    )(samples.reshape(SUBS, CHUNK, samples.shape[1]))
    return out.reshape(-1, PAIR)


def solution(mesh):
    return jax.shard_map(
        body, mesh=mesh, in_specs=(P(("row", "pair"), None),), out_specs=P("row", "pair"), check_vma=False
    )
```

```python
import functools

import jax
import jax.numpy as jnp
from jax import lax
from jax.experimental import pallas as pl
from jax.experimental.pallas import tpu as pltpu
from jax.sharding import PartitionSpec as P

MESH = pl.DeviceIdType.MESH
F32 = jnp.float32
BF16 = jnp.bfloat16
NS_STEPS = 5
ROWS = 32768
CHIPS = 16
PEERS = CHIPS - 1
SUBS = 4
CHUNK = 64
PAIR = 512
HALF = 256
PACKED = 3 * HALF
CORE_PART = PACKED // 2
QUARTER = CORE_PART // 4
SENDS = 2 * SUBS * PEERS
WINDOW = SUBS * PEERS
SHARED = 2


def dot(left, right, dims=((1,), (0,))):
    return lax.dot_general(left, right, (dims, ((), ())), preferred_element_type=F32)


def split(ref_hi, ref_lo, value):
    high = value.astype(BF16)
    ref_hi[...] = high
    ref_lo[...] = (value - high.astype(F32)).astype(BF16)


def product(left, right, fine=True):
    lh, ll = left
    rh, rl = right
    if not fine:
        return dot(lh[...], rh[...])
    return dot(lh[...], rh[...]) + (dot(lh[...], rl[...]) + dot(ll[...], rh[...]))


def kernel(
    x_ref, o_ref,
    y, part, from_core, from_quarter, full, zmat, mmat, zh, zl, mh, ml, th, tl, rot, w_send, w_keep, shared, w_shared,
    own_sem, a2a_send, a2a_recv, core_send, core_recv, rs_send, rs_recv, ag_send, ag_recv,
    back_send, back_recv, w_send_sem, w_recv_sem, w_keep_sem, share_send, share_recv, w_shared_sem,
):
    row = lax.axis_index("row")
    pair = lax.axis_index("pair")
    core = lax.rem(row, 2)
    x_hi = row // 2
    plane = lax.rem(pair, 2)
    chip = pair // 2
    y_pos, z_pos = chip // 4, lax.rem(chip, 4)
    quarter = x_hi * 2 + plane

    def member(stage, step):
        other = lax.rem(quarter + step, 4)
        other_plane = lax.rem(other, 2)
        other_chip = chip
        if stage == 1:
            other_chip = lax.rem(chip + plane - other_plane + CHIPS, CHIPS)
        return other, ((other // 2) * 2 + core, other_chip * 2 + other_plane)

    core_peer = (x_hi * 2 + 1 - core, pair)

    def partner(stage):
        other_chip = chip
        if stage == 1:
            other_chip = lax.rem(chip + 2 * plane - 1 + CHIPS, CHIPS)
        return (row, other_chip * 2 + 1 - plane)

    barrier = pltpu.get_barrier_semaphore()

    def greet(device):
        pl.semaphore_signal(barrier, inc=1, device_id=device, device_id_type=MESH)

    def offset(i):
        turn = 1 + lax.rem(i * 7, PEERS)
        return lax.rem(y_pos + turn // 4, 4) * 4 + lax.rem(z_pos + lax.rem(turn, 4), 4)

    def greet_plane(i, carry):
        greet((row, offset(i) * 2 + plane))
        return carry

    lax.fori_loop(0, PEERS, greet_plane, 0)
    greet(core_peer)
    for step in range(1, 4):
        greet(member(0, step)[1])
    greet(member(1, 1)[1])
    greet(member(1, 3)[1])

    def columns_of(stage, target):
        index = 2 * target
        if not isinstance(stage, int):
            index = index + stage * (2 * plane - 1)
        elif stage == 1:
            index = index + 2 * plane - 1
        index = lax.rem(index + 2 * CHIPS, 2 * CHIPS)
        return pl.ds(pl.multiple_of(index * PAIR, PAIR), PAIR)

    def own_copy(stage):
        return pltpu.make_async_copy(
            x_ref.at[:, :, columns_of(stage, chip)], y.at[stage, :, chip], own_sem.at[stage]
        )

    for stage in range(2):
        own_copy(stage).start()
    pl.semaphore_wait(barrier, PEERS + 6)

    def a2a_copy(n):
        phase, i = n // PEERS, lax.rem(n, PEERS)
        stage, sub = phase // SUBS, lax.rem(phase, SUBS)
        target = offset(i)
        return pltpu.make_async_remote_copy(
            src_ref=x_ref.at[sub, :, columns_of(stage, target)],
            dst_ref=y.at[stage, sub, chip],
            send_sem=a2a_send.at[lax.rem(n, WINDOW)],
            recv_sem=a2a_recv.at[phase],
            device_id=(row, target * 2 + plane),
            device_id_type=MESH,
        )

    def a2a_first(n, carry):
        a2a_copy(n).start()
        return carry

    def a2a_next(n, carry):
        a2a_copy(n - WINDOW).wait_send()
        a2a_copy(n).start()
        return carry

    sent = [0]

    def pump(count):
        stop = min(SENDS, sent[0] + count)
        if stop > sent[0]:
            lax.fori_loop(sent[0], stop, a2a_next, 0)
            sent[0] = stop

    def a2a_arrived(stage, sub):
        landed = y.at[stage, sub, pl.ds(0, PEERS)]
        pltpu.make_async_copy(landed, landed, a2a_recv.at[stage * SUBS + sub]).wait()

    def gram(stage, sub):
        rows = y[stage, sub].reshape(CHIPS * CHUNK, PAIR)
        left, right = rows[:, :HALF], rows[:, HALF:]
        for index, (one, two) in enumerate(((left, left), (left, right), (right, right))):
            here = pl.ds(index * HALF, HALF)
            term = dot(one, two, ((0,), (0,)))
            if sub == 0:
                part[stage, here] = term
            else:
                part[stage, here] += term

    core_rows = pl.ds(pl.multiple_of(core * CORE_PART, CORE_PART), CORE_PART)
    peer_rows = pl.ds(pl.multiple_of((1 - core) * CORE_PART, CORE_PART), CORE_PART)

    def quarter_rows(which):
        return pl.ds(pl.multiple_of(core * CORE_PART + which * QUARTER, QUARTER), QUARTER)

    def core_copy(stage):
        return pltpu.make_async_remote_copy(
            src_ref=part.at[stage, peer_rows], dst_ref=from_core.at[stage],
            send_sem=core_send.at[stage], recv_sem=core_recv.at[stage],
            device_id=core_peer, device_id_type=MESH,
        )

    def rs_copy(stage, step):
        other, device = member(stage, step)
        return pltpu.make_async_remote_copy(
            src_ref=part.at[stage, quarter_rows(other)], dst_ref=from_quarter.at[stage, step - 1],
            send_sem=rs_send.at[stage, step - 1], recv_sem=rs_recv.at[stage, step - 1],
            device_id=device, device_id_type=MESH,
        )

    def ag_copy(stage, step):
        _, device = member(stage, step)
        return pltpu.make_async_remote_copy(
            src_ref=full.at[stage, quarter_rows(quarter)], dst_ref=full.at[stage, quarter_rows(quarter)],
            send_sem=ag_send.at[stage, step - 1], recv_sem=ag_recv.at[stage, step - 1],
            device_id=device, device_id_type=MESH,
        )

    def back_copy(stage):
        return pltpu.make_async_remote_copy(
            src_ref=full.at[stage, core_rows], dst_ref=full.at[stage, core_rows],
            send_sem=back_send.at[stage], recv_sem=back_recv.at[stage],
            device_id=core_peer, device_id_type=MESH,
        )

    def reduce_1(stage):
        core_copy(stage).start()

    def reduce_2(stage):
        core_copy(stage).wait_recv()
        part[stage, core_rows] += from_core[stage]
        for step in (2, 1, 3):
            rs_copy(stage, step).start()

    def reduce_3(stage):
        total = part[stage, quarter_rows(quarter)]
        for step in (1, 3, 2):
            rs_copy(stage, step).wait_recv()
            total = total + from_quarter[stage, step - 1]
        full[stage, quarter_rows(quarter)] = total
        for step in (2, 1, 3):
            ag_copy(stage, step).start()

    def reduce_4(stage):
        for step in (1, 3, 2):
            ag_copy(stage, step).wait_recv()
        back_copy(stage).start()

    def reduce_5(stage):
        back_copy(stage).wait_recv()
        for step in range(1, 4):
            rs_copy(stage, step).wait_send()
            ag_copy(stage, step).wait_send()
        core_copy(stage).wait_send()
        back_copy(stage).wait_send()

    diagonal = lambda: (
        lax.broadcasted_iota(jnp.int32, (PAIR, PAIR), 0) == lax.broadcasted_iota(jnp.int32, (PAIR, PAIR), 1)
    ).astype(F32)

    def newton(stage):
        g00 = full[stage, pl.ds(0, HALF)]
        g01 = full[stage, pl.ds(HALF, HALF)]
        g11 = full[stage, pl.ds(2 * HALF, HALF)]
        square = (
            jnp.sum(g00 * g00, keepdims=True) + 2.0 * jnp.sum(g01 * g01, keepdims=True)
            + jnp.sum(g11 * g11, keepdims=True)
        )
        norm = jnp.sqrt(square)
        mmat[:HALF, :HALF] = g00 / norm
        mmat[:HALF, HALF:] = g01 / norm
        mmat[HALF:, :HALF] = (g01 / norm).T
        mmat[HALF:, HALF:] = g11 / norm
        split(mh, ml, mmat[...])
        zmat[...] = 1.5 * diagonal() - 0.5 * mmat[...]
        mmat[...] = 1.5 * mmat[...] - 0.5 * product((mh, ml), (mh, ml), False)
        split(zh, zl, zmat[...])
        split(mh, ml, mmat[...])
        for step in range(1, NS_STEPS - 1):
            fine = step >= NS_STEPS - 1
            split(th, tl, product((zh, zl), (mh, ml), fine))
            mmat[...] = 1.5 * mmat[...] - 0.5 * product((mh, ml), (th, tl), fine)
            zmat[...] = 1.5 * zmat[...] - 0.5 * product((th, tl), (zh, zl), fine)
            split(zh, zl, zmat[...])
            split(mh, ml, mmat[...])
        split(th, tl, product((zh, zl), (mh, ml)))
        last = 1.5 * zmat[...] - 0.5 * product((th, tl), (zh, zl))
        rot[stage] = (last * jnp.sqrt(ROWS / norm)).astype(BF16)

    def half_of(stage, kept):
        which = plane if (stage == 0) == kept else 1 - plane
        return pl.ds(pl.multiple_of(which * HALF, HALF), HALF)

    def send_copy(stage, sub):
        return pltpu.make_async_remote_copy(
            src_ref=w_send.at[stage, sub],
            dst_ref=o_ref.at[:, plane, sub, :, half_of(stage, False)],
            send_sem=w_send_sem.at[stage, sub], recv_sem=w_recv_sem.at[stage, sub],
            device_id=partner(stage), device_id_type=MESH,
        )

    def keep_copy(stage, sub):
        return pltpu.make_async_copy(
            w_keep.at[stage, sub],
            o_ref.at[:, plane, sub, :, half_of(stage, True)],
            w_keep_sem.at[stage, sub],
        )

    def share_copy(sub):
        return pltpu.make_async_remote_copy(
            src_ref=y.at[0, sub], dst_ref=shared.at[sub],
            send_sem=share_send.at[sub], recv_sem=share_recv.at[sub],
            device_id=partner(0), device_id_type=MESH,
        )

    def shared_keep_copy(sub):
        return pltpu.make_async_copy(
            w_shared.at[sub],
            o_ref.at[:, 1 - plane, sub, :, half_of(0, True)],
            w_shared_sem.at[sub],
        )

    def apply_shared(sub):
        share_copy(sub).wait_recv()
        rows = shared[sub].reshape(CHIPS * CHUNK, PAIR)
        value = dot(rows, rot[0, :, half_of(0, True)]).astype(BF16)
        w_shared[sub] = value.reshape(CHIPS, CHUNK, HALF)
        shared_keep_copy(sub).start()

    def apply(stage, sub, kept):
        rows = y[stage, sub].reshape(CHIPS * CHUNK, PAIR)
        value = dot(rows, rot[stage, :, half_of(stage, kept)]).astype(BF16)
        (w_keep if kept else w_send)[stage, sub] = value.reshape(CHIPS, CHUNK, HALF)
        (keep_copy if kept else send_copy)(stage, sub).start()

    lax.fori_loop(0, WINDOW, a2a_first, 0)
    sent[0] = WINDOW
    for sub in range(SUBS):
        pump(PEERS)
        if sub == 0:
            own_copy(0).wait()
        a2a_arrived(0, sub)
        if sub < SHARED:
            share_copy(sub).start()
        gram(0, sub)
    reduce_1(0)
    reduce_2(0)
    reduce_3(0)
    reduce_4(0)
    reduce_5(0)
    newton(0)
    apply(0, 2, False)
    own_copy(1).wait()
    for sub in range(SUBS):
        a2a_arrived(1, sub)
        gram(1, sub)
        if sub < SUBS - 1:
            apply(0, sub, True)
    reduce_1(1)
    apply(0, SUBS - 1, True)
    reduce_2(1)
    apply_shared(0)
    reduce_3(1)
    apply(0, 3, False)
    apply_shared(1)
    reduce_4(1)
    reduce_5(1)
    newton(1)
    for sub in range(SUBS):
        apply(1, sub, False)
    for sub in range(SUBS):
        apply(1, sub, True)

    def a2a_drain(n, carry):
        a2a_copy(n).wait_send()
        return carry

    lax.fori_loop(SENDS - WINDOW, SENDS, a2a_drain, 0)
    for stage in range(2):
        for sub in range(SUBS):
            if stage == 1 or sub >= SHARED:
                send_copy(stage, sub).wait()
            keep_copy(stage, sub).wait()
    for sub in range(SHARED):
        share_copy(sub).wait_send()
        shared_keep_copy(sub).wait()


def body(samples):
    sems = lambda *shape: pltpu.SemaphoreType.DMA(shape)
    square = (PAIR, PAIR)
    out = pl.pallas_call(
        kernel,
        out_shape=jax.ShapeDtypeStruct((CHIPS, 2, SUBS, CHUNK, PAIR), BF16),
        in_specs=[pl.BlockSpec(memory_space=pl.ANY)],
        out_specs=pl.BlockSpec(memory_space=pl.ANY),
        scratch_shapes=[
            pltpu.VMEM((2, SUBS, CHIPS, CHUNK, PAIR), BF16),
            pltpu.VMEM((2, PACKED, HALF), F32),
            pltpu.VMEM((2, CORE_PART, HALF), F32),
            pltpu.VMEM((2, 3, QUARTER, HALF), F32),
            pltpu.VMEM((2, PACKED, HALF), F32),
            pltpu.VMEM(square, F32), pltpu.VMEM(square, F32),
            *[pltpu.VMEM(square, BF16)] * 6,
            pltpu.VMEM((2, *square), BF16),
            pltpu.VMEM((2, SUBS, CHIPS, CHUNK, HALF), BF16),
            pltpu.VMEM((2, SUBS, CHIPS, CHUNK, HALF), BF16),
            pltpu.VMEM((SHARED, CHIPS, CHUNK, PAIR), BF16),
            pltpu.VMEM((SHARED, CHIPS, CHUNK, HALF), BF16),
            sems(2), sems(WINDOW), sems(2 * SUBS), sems(2), sems(2), sems(2, 3), sems(2, 3), sems(2, 3), sems(2, 3),
            sems(2), sems(2), sems(2, SUBS), sems(2, SUBS), sems(2, SUBS),
            sems(SHARED), sems(SHARED), sems(SHARED),
        ],
        compiler_params=pltpu.CompilerParams(
            collective_id=0, has_side_effects=True, vmem_limit_bytes=56 * 2**20
        ),
    )(samples.reshape(SUBS, CHUNK, samples.shape[1]))
    return out.reshape(-1, PAIR)


def solution(mesh):
    return jax.shard_map(
        body, mesh=mesh, in_specs=(P(("row", "pair"), None),), out_specs=P("row", "pair"), check_vma=False
    )
```
